32 devices in a mesh: dp: 2 (over x), width: 4 (over y, core), hidden: 4 (over z).
Axes of the slice: x: 2, y: 2, z: 4, core: 2. Of those that a mesh axis runs over, the one named last changes fastest.
Arguments:
- tokens: bfloat16 [1024, 8192], P('dp', 'width'), may hold values from -6 to 6
- target: bfloat16 [1024, 8192], P('dp', 'width'), may hold values from -6 to 6
- gate_weight: bfloat16 [8192, 14336], P('width', 'hidden'), may hold values from -0.0625 to 0.0625
- up_weight: bfloat16 [8192, 14336], P('width', 'hidden'), may hold values from -0.0625 to 0.0625
- down_weight: bfloat16 [14336, 8192], P('hidden', 'width'), may hold values from -0.046875 to 0.046875
- probe_sign: bfloat16 [8192, 14336], P('width', 'hidden'), may hold values from -1 to 1, as said below
Outputs:
- gate_grad: bfloat16 [8192, 14336], P(('width', 'dp'), 'hidden')
- hess_diag: bfloat16 [8192, 14336], P(('width', 'dp'), 'hidden')
The draws below stay inside these ranges and needn't reach their ends.
Inputs may be any that keep to these rules, and one draw needn't show every extreme that they name: `probe_sign`: every entry is -1 or +1.
All inputs are finite; a program needn't handle non-finite values.
Results may differ from the reference program's by a relative error of at most 0.019.
Values may be sent and summed in bfloat16 or wider, within the bound.
A program may use at most 192 MiB of HBM per device.

```python
import math
import jax
import jax.numpy as jnp

D = 8192
FF = 14336
TOK_DEV = 512
TOKENS = 1024
N_DP = 2


def draw_probe_sign(key, part):
    coin_bits = jax.random.randint(key, (D, FF), 0, 2)
    return (2 * coin_bits - 1).astype(jnp.bfloat16)


def block_scale(rng, extent, shards, least, high):
    def one(axis_at, blocks):
        draws = jax.random.uniform(jax.random.fold_in(jax.random.fold_in(rng, 6), axis_at), (blocks,), jnp.float32, least / len(shards), high / len(shards))
        return jnp.repeat(jnp.exp(draws), extent[axis_at] // blocks).reshape((-1,) + (1,) * (len(extent) - axis_at - 1))

    gain = one(*shards[0])
    for cut in shards[1:]:
        gain = gain * one(*cut)
    return gain


def gaussian(own_key, extent, deviation, reach, split=(), dtype=jnp.bfloat16):
    result = deviation * jax.random.normal(own_key, extent, jnp.float32)
    if split:
        result = result * block_scale(own_key, extent, split, -0.22, 0.18)
    return jnp.clip(result, -reach, reach).astype(dtype)


def setup_inputs(seed: int = 0) -> dict:
    keys = jax.random.split(jax.random.key(seed), 7)
    return {
        "tokens": gaussian(keys[0], (TOKENS, D), 1.0, 6.0, ((0, 2), (1, 4))),
        "target": gaussian(keys[1], (TOKENS, D), 1.0, 6.0, ((0, 2), (1, 4))),
        "gate_weight": gaussian(keys[2], (D, FF), D ** -0.5, 0.0625, ((0, 4), (1, 4))),
        "up_weight": gaussian(keys[3], (D, FF), D ** -0.5, 0.0625, ((0, 4), (1, 4))),
        "down_weight": gaussian(keys[4], (FF, D), FF ** -0.5, 0.046875, ((0, 4), (1, 4))),
        "probe_sign": draw_probe_sign(jax.random.fold_in(keys[6], 71), 0),
    }


def reference(tokens, target, gate_weight, up_weight, down_weight, probe_sign):
    inv_width = 1.0 / math.sqrt(D)
    token_scale = 1.0 / math.sqrt(TOKENS)
    gate_pre = jnp.dot(tokens, gate_weight, preferred_element_type=jnp.float32)
    up_pre = jnp.dot(tokens, up_weight, preferred_element_type=jnp.float32)
    tangent = jnp.dot(tokens, probe_sign, preferred_element_type=jnp.float32) * inv_width
    sigmoid_gate = jax.nn.sigmoid(gate_pre)
    first = sigmoid_gate * (1.0 + gate_pre * (1.0 - sigmoid_gate))
    second = sigmoid_gate * (1.0 - sigmoid_gate) * (2.0 + gate_pre * (1.0 - 2.0 * sigmoid_gate))
    hidden = (gate_pre * sigmoid_gate * up_pre).astype(jnp.bfloat16)
    hidden_dot = (first * tangent * up_pre).astype(jnp.bfloat16)
    coeff_first = (first * up_pre).astype(jnp.bfloat16)
    coeff_second = (second * tangent * up_pre).astype(jnp.bfloat16)
    output = jnp.dot(hidden, down_weight, preferred_element_type=jnp.float32)
    output_dot = jnp.dot(hidden_dot, down_weight, preferred_element_type=jnp.float32)
    resid = (output - target.astype(jnp.float32)).astype(jnp.bfloat16)
    output_dot_b = output_dot.astype(jnp.bfloat16)
    back = jnp.dot(resid, down_weight.T, preferred_element_type=jnp.float32)
    back_dot = jnp.dot(output_dot_b, down_weight.T, preferred_element_type=jnp.float32)
    err_grad = (back * coeff_first.astype(jnp.float32)).astype(jnp.bfloat16)
    err_hess = (back * coeff_second.astype(jnp.float32) + back_dot * coeff_first.astype(jnp.float32)).astype(jnp.bfloat16)
    grad_sum = jnp.zeros((D, FF), jnp.float32)
    hv_sum = jnp.zeros((D, FF), jnp.float32)
    for half in range(N_DP):
        lower = half * TOK_DEV
        tok_half = tokens[lower:lower + TOK_DEV]
        grad_part = jnp.dot(tok_half.T, err_grad[lower:lower + TOK_DEV], preferred_element_type=jnp.float32) * token_scale
        hv_part = jnp.dot(tok_half.T, err_hess[lower:lower + TOK_DEV], preferred_element_type=jnp.float32) * token_scale
        grad_sum = grad_sum + grad_part.astype(jnp.bfloat16).astype(jnp.float32)
        hv_sum = hv_sum + hv_part.astype(jnp.bfloat16).astype(jnp.float32)
    gate_grad = grad_sum.astype(jnp.bfloat16)
    hess_diag = (probe_sign.astype(jnp.float32) * hv_sum * inv_width).astype(jnp.bfloat16)
    return (gate_grad, hess_diag)
```

```python
import math

import jax
import jax.numpy as jnp
from jax import lax
from jax.sharding import PartitionSpec as P

D = 8192
CHUNKS = 2
BF16 = jnp.bfloat16
F32 = jnp.float32


def matmul(left, right, dims=((1,), (0,)), out=BF16):
    return lax.dot_general(left, right, (dims, ((), ())), preferred_element_type=F32).astype(out)


def shift_core(x):
    n = lax.axis_size("width")
    return lax.ppermute(x, "width", [(i, i ^ 1) for i in range(n)])


def shift_y(x):
    n = lax.axis_size("width")
    return lax.ppermute(x, "width", [(i, (i + 2) % n) for i in range(n)])


def shift_z(x, step):
    n = lax.axis_size("hidden")
    return lax.ppermute(x, "hidden", [(i, (i + step) % n) for i in range(n)])


def shift_dp(x):
    n = lax.axis_size("dp")
    return lax.ppermute(x, "dp", [(i, (i + 1) % n) for i in range(n)])


def add(left, right):
    return left.astype(F32) + right.astype(F32)


def reduce_width(x):
    ny = x.shape[0]
    x = add(x[:, 0], shift_core(x[:, 1]))
    total = x[ny - 1]
    for step in range(ny - 1):
        total = add(x[ny - 2 - step], shift_y(total.astype(BF16)))
    return total


def gather_width(x, ny):
    pieces = [None] * ny
    pieces[0] = x
    for step in range(ny - 1):
        x = shift_y(x)
        pieces[ny - 1 - step] = x
    return pieces


def reduce_hidden(x, step):
    n = len(x)
    at = (-step) % n
    total = x[at]
    for _ in range(n - 1):
        at = (at - step) % n
        total = add(x[at], shift_z(total.astype(BF16), step))
    return total


def gather_hidden(x, step, n):
    pieces = [None] * n
    pieces[0] = x
    at = 0
    for _ in range(n - 1):
        at = (at - step) % n
        x = shift_z(x, step)
        pieces[at] = x
    return pieces


def coefficients(gate_pre, up_pre, tangent):
    sigmoid_gate = jax.nn.sigmoid(gate_pre)
    first = sigmoid_gate * (1.0 + gate_pre * (1.0 - sigmoid_gate))
    second = sigmoid_gate * (1.0 - sigmoid_gate) * (2.0 + gate_pre * (1.0 - 2.0 * sigmoid_gate))
    hidden = (gate_pre * sigmoid_gate * up_pre).astype(BF16)
    hidden_dot = (first * tangent * up_pre).astype(BF16)
    coeff_first = (first * up_pre).astype(BF16)
    coeff_second = (second * tangent * up_pre).astype(BF16)
    return (hidden, hidden_dot, coeff_first, coeff_second)


def errors(back, back_dot, coeff_first, coeff_second):
    first_f = coeff_first.astype(F32)
    err_grad = (back * first_f).astype(BF16)
    err_hess = (back * coeff_second.astype(F32) + back_dot * first_f).astype(BF16)
    return (err_grad, err_hess)


def on_device(tokens, target, gate_weight, up_weight, down_weight, probe_sign):
    inv_width = 1.0 / math.sqrt(D)
    n_dp = lax.axis_size("dp")
    n_width = lax.axis_size("width")
    nz = lax.axis_size("hidden")
    ny = n_width // 2
    rows, cols = tokens.shape
    ff = gate_weight.shape[1]
    token_scale = 1.0 / math.sqrt(rows * n_dp)
    half = cols // n_dp
    t = rows // CHUNKS
    r = t // (n_width * nz)
    dp = lax.axis_index("dp")
    w = lax.axis_index("width")
    z = lax.axis_index("hidden")

    row = lax.broadcasted_iota(jnp.int32, (rows, rows), 0)
    col = lax.broadcasted_iota(jnp.int32, (rows, rows), 1)
    sz = (row // r) % nz
    pc = (row // (r * nz)) % 2
    py = (row // (r * nz * 2)) % ny
    source = (
        (row // t) * t
        + ((((py + w // 2) % ny) * 2 + (pc + w % 2) % 2) * nz + (sz + z) % nz) * r
        + row % r
    )
    order = (source == col).astype(BF16)
    tokens = matmul(order, tokens)
    target = matmul(order, target)
    mine = lax.dynamic_slice_in_dim(tokens, dp * half, half, 1)
    other = shift_dp(lax.dynamic_slice_in_dim(tokens, (1 - dp) * half, half, 1))

    def stage_a(k):
        tok = tokens[k * t:(k + 1) * t]
        pre = [
            reduce_width(matmul(tok, weight).reshape(ny, 2, nz * r, ff))
            for weight in (gate_weight, up_weight, probe_sign)
        ]
        hidden, hidden_dot, c1, c2 = coefficients(pre[0], pre[1], pre[2] * inv_width)
        both = jnp.stack([hidden, hidden_dot])
        own = jnp.stack(gather_width(both, ny), axis=1)
        full = jnp.stack([own, shift_core(own)], axis=2)
        return full.reshape(2 * t, ff), c1, c2

    def stage_b(k, full):
        out = matmul(full, down_weight).reshape(2, n_width, nz, r, cols)
        result = []
        for i, step in ((0, 1), (1, -1)):
            total = reduce_hidden([out[i, :, s] for s in range(nz)], step)
            if i == 0:
                goal = target[k * t:(k + 1) * t].reshape(n_width, nz, r, cols)[:, 0]
                total = total - goal.astype(F32)
            pieces = gather_hidden(total.astype(BF16), step, nz)
            result.append(jnp.stack(pieces, axis=1).reshape(t, cols))
        return result

    def stage_c(resid, output_dot, c1, c2):
        back, back_dot = [
            reduce_width(matmul(v, down_weight, ((1,), (1,))).reshape(ny, 2, nz * r, ff))
            for v in (resid, output_dot)
        ]
        result = []
        for err in errors(back, back_dot, c1, c2):
            own = gather_width(err, ny)
            far = [shift_dp(piece) for piece in own]
            part = jnp.stack(own + far)
            result.append(jnp.stack([part, shift_core(part)], axis=1).reshape(n_dp * t, ff))
        return result

    a = [stage_a(k) for k in range(CHUNKS)]
    b = [stage_b(k, a[k][0]) for k in range(CHUNKS)]
    c = [stage_c(*b[k], a[k][1], a[k][2]) for k in range(CHUNKS)]
    sums = [None, None]
    for k in range(CHUNKS):
        tok = jnp.concatenate([mine[k * t:(k + 1) * t], other[k * t:(k + 1) * t]])
        for i in range(2):
            term = matmul(tok, c[k][i], ((0,), (0,)), F32)
            sums[i] = term if sums[i] is None else sums[i] + term
    probe_rows = lax.dynamic_slice_in_dim(probe_sign, dp * half, half, 0)
    gate_grad = (sums[0] * token_scale).astype(BF16)
    hess_diag = (probe_rows.astype(F32) * (sums[1] * token_scale) * inv_width).astype(BF16)
    return (gate_grad, hess_diag)


def solution(mesh):
    return jax.shard_map(
        on_device,
        mesh=mesh,
        in_specs=(
            P("dp", "width"),
            P("dp", "width"),
            P("width", "hidden"),
            P("width", "hidden"),
            P("hidden", "width"),
            P("width", "hidden"),
        ),
        out_specs=(P(("width", "dp"), "hidden"), P(("width", "dp"), "hidden")),
        check_vma=False,
    )
```

```python
import math

import jax
import jax.numpy as jnp
from jax import lax
from jax.experimental import pallas as pl
from jax.experimental.pallas import tpu as pltpu
from jax.sharding import PartitionSpec as P

D = 8192
CHUNKS = 2
BF16 = jnp.bfloat16
F32 = jnp.float32


def matmul(left, right, dims=((1,), (0,)), out=BF16):
    return lax.dot_general(left, right, (dims, ((), ())), preferred_element_type=F32).astype(out)


def after(x, *others):
    return lax.optimization_barrier((x, others))[0]


def back_kernel(left_ref, right_ref, out_ref):
    out_ref[...] = lax.dot_general(
        left_ref[...], right_ref[...], (((1,), (1,)), ((), ())), preferred_element_type=F32
    ).astype(out_ref.dtype)


def matmul_back(left, right):
    (m, depth), n = left.shape, right.shape[0]
    tile = 512 if n % 512 == 0 else 256
    return pl.pallas_call(
        back_kernel,
        grid=(n // tile,),
        in_specs=[
            pl.BlockSpec((m, depth), lambda i: (0, 0)),
            pl.BlockSpec((tile, depth), lambda i: (i, 0)),
        ],
        out_specs=pl.BlockSpec((m, tile), lambda i: (0, i)),
        out_shape=jax.ShapeDtypeStruct((m, n), BF16),
        compiler_params=pltpu.CompilerParams(vmem_limit_bytes=24 * 1024 * 1024),
        cost_estimate=pl.CostEstimate(
            flops=2 * m * n * depth,
            bytes_accessed=2 * (m * depth + n * depth + m * n),
            transcendentals=0,
        ),
    )(left, right)


def shift_core(x):
    n = lax.axis_size("width")
    return lax.ppermute(x, "width", [(i, i ^ 1) for i in range(n)])


def shift_y(x):
    n = lax.axis_size("width")
    return lax.ppermute(x, "width", [(i, (i + 2) % n) for i in range(n)])


def shift_z(x, step):
    n = lax.axis_size("hidden")
    return lax.ppermute(x, "hidden", [(i, (i + step) % n) for i in range(n)])


def shift_dp(x):
    n = lax.axis_size("dp")
    return lax.ppermute(x, "dp", [(i, (i + 1) % n) for i in range(n)])


def add(left, right):
    return left.astype(F32) + right.astype(F32)


def reduce_core(x):
    return add(x[:, 0], shift_core(x[:, 1]))


def reduce_y(x):
    ny = x.shape[0]
    total = x[ny - 1]
    for step in range(ny - 1):
        total = add(x[ny - 2 - step], shift_y(total.astype(BF16)))
    return total


def gather_width(x, ny):
    pieces = [None] * ny
    pieces[0] = x
    for step in range(ny - 1):
        x = shift_y(x)
        pieces[ny - 1 - step] = x
    return pieces


def reduce_hidden(x, step):
    n = len(x)
    at = (-step) % n
    total = x[at]
    for _ in range(n - 1):
        at = (at - step) % n
        total = add(x[at], shift_z(total.astype(BF16), step))
    return total


def gather_hidden(x, step, n):
    pieces = [None] * n
    pieces[0] = x
    at = 0
    for _ in range(n - 1):
        at = (at - step) % n
        x = shift_z(x, step)
        pieces[at] = x
    return pieces


def coefficients(gate_pre, up_pre, tangent):
    sigmoid_gate = jax.nn.sigmoid(gate_pre)
    first = sigmoid_gate * (1.0 + gate_pre * (1.0 - sigmoid_gate))
    second = sigmoid_gate * (1.0 - sigmoid_gate) * (2.0 + gate_pre * (1.0 - 2.0 * sigmoid_gate))
    hidden = (gate_pre * sigmoid_gate * up_pre).astype(BF16)
    hidden_dot = (first * tangent * up_pre).astype(BF16)
    coeff_first = (first * up_pre).astype(BF16)
    coeff_second = (second * tangent * up_pre).astype(BF16)
    return (hidden, hidden_dot, coeff_first, coeff_second)


def errors(back, back_dot, coeff_first, coeff_second):
    first_f = coeff_first.astype(F32)
    err_grad = (back * first_f).astype(BF16)
    err_hess = (back * coeff_second.astype(F32) + back_dot * first_f).astype(BF16)
    return (err_grad, err_hess)


def on_device(tokens, target, gate_weight, up_weight, down_weight, probe_sign):
    inv_width = 1.0 / math.sqrt(D)
    n_dp = lax.axis_size("dp")
    n_width = lax.axis_size("width")
    nz = lax.axis_size("hidden")
    ny = n_width // 2
    rows, cols = tokens.shape
    ff = gate_weight.shape[1]
    token_scale = 1.0 / math.sqrt(rows * n_dp)
    half = cols // n_dp
    t = rows // CHUNKS
    r = t // (n_width * nz)
    dp = lax.axis_index("dp")
    w = lax.axis_index("width")
    z = lax.axis_index("hidden")

    row = lax.broadcasted_iota(jnp.int32, (rows, rows), 0)
    col = lax.broadcasted_iota(jnp.int32, (rows, rows), 1)
    sz = (row // r) % nz
    pc = (row // (r * nz)) % 2
    py = (row // (r * nz * 2)) % ny
    source = (
        (row // t) * t
        + ((((py + w // 2) % ny) * 2 + (pc + w % 2) % 2) * nz + (sz + z) % nz) * r
        + row % r
    )
    order = (source == col).astype(BF16)
    tokens = matmul(order, tokens)
    target = matmul(order, target)
    mine = lax.dynamic_slice_in_dim(tokens, dp * half, half, 1)
    other = shift_dp(lax.dynamic_slice_in_dim(tokens, (1 - dp) * half, half, 1))

    def stage_a(tok):
        chip = []
        for weight in (gate_weight, up_weight, probe_sign):
            held = after(tok, chip[0]) if len(chip) == 2 else tok
            chip.append(reduce_core(matmul(held, weight).reshape(ny, 2, nz * r, ff)))
        pre = [reduce_y(part) for part in chip]
        hidden, hidden_dot, c1, c2 = coefficients(pre[0], pre[1], pre[2] * inv_width)
        both = jnp.stack([hidden, hidden_dot])
        own = jnp.stack(gather_width(both, ny), axis=1)
        full = jnp.stack([own, shift_core(own)], axis=2)
        return full.reshape(2 * t, ff), c1, c2, pre[2]

    def stage_b(k, out):
        out = out.reshape(2, n_width, nz, r, cols)
        result, totals = [], []
        for i, step in ((0, 1), (1, -1)):
            total = reduce_hidden([out[i, :, s] for s in range(nz)], step)
            if i == 0:
                goal = target[k * t:(k + 1) * t].reshape(n_width, nz, r, cols)[:, 0]
                total = total - goal.astype(F32)
            total = total.astype(BF16)
            totals.append(total)
            pieces = gather_hidden(total, step, nz)
            result.append(jnp.stack(pieces, axis=1).reshape(t, cols))
        return jnp.concatenate(result), totals

    def stage_c(resid, c1, c2):
        back = matmul_back(resid, down_weight).reshape(2, ny, 2, nz * r, ff)
        return errors(reduce_y(reduce_core(back[0])), reduce_y(reduce_core(back[1])), c1, c2)

    def gather_error(err, y_last):
        own = gather_width(err, ny)
        if y_last:
            far = gather_width(shift_dp(err), ny)
        else:
            far = [shift_dp(piece) for piece in own]
        part = jnp.stack(own + far)
        return jnp.stack([part, shift_core(part)], axis=1).reshape(n_dp * t, ff)

    coeffs, fulls, resids, gathered = [], [], [], []
    totals = mark = err = None
    for k in range(CHUNKS):
        tok = tokens[k * t:(k + 1) * t]
        if k:
            tok = after(tok, mark)
        full, c1, c2, mark = stage_a(tok)
        fulls.append(full)
        coeffs.append((c1, c2))
    for k in range(CHUNKS):
        full = after(fulls[k], *totals) if k else fulls[k]
        out = matmul(full, down_weight)
        if k:
            out = after(out, resids[-1])
        resid, totals = stage_b(k, out)
        resids.append(resid)
    for k in range(CHUNKS):
        resid = after(resids[k], *err) if k else resids[k]
        err = stage_c(resid, *coeffs[k])
        gathered.append([gather_error(err[i], k == CHUNKS - 1 and i == 1) for i in range(2)])
    tok = jnp.concatenate(
        [part[k * t:(k + 1) * t] for k in range(CHUNKS) for part in (mine, other)]
    )
    sums = [
        matmul(tok, jnp.concatenate([g[i] for g in gathered]), ((0,), (0,)), F32)
        for i in range(2)
    ]
    probe_rows = lax.dynamic_slice_in_dim(probe_sign, dp * half, half, 0)
    gate_grad = (sums[0] * token_scale).astype(BF16)
    hess_diag = (probe_rows.astype(F32) * (sums[1] * token_scale) * inv_width).astype(BF16)
    return (gate_grad, hess_diag)


def solution(mesh):
    return jax.shard_map(
        on_device,
        mesh=mesh,
        in_specs=(
            P("dp", "width"),
            P("dp", "width"),
            P("width", "hidden"),
            P("width", "hidden"),
            P("hidden", "width"),
            P("width", "hidden"),
        ),
        out_specs=(P(("width", "dp"), "hidden"), P(("width", "dp"), "hidden")),
        check_vma=False,
    )
```

```python
import math

import jax
import jax.numpy as jnp
from jax import lax
from jax.experimental import pallas as pl
from jax.experimental.pallas import tpu as pltpu
from jax.sharding import PartitionSpec as P

D = 8192
CHUNKS = 2
BF16 = jnp.bfloat16
F32 = jnp.float32


def matmul(left, right, dims=((1,), (0,)), out=BF16):
    return lax.dot_general(left, right, (dims, ((), ())), preferred_element_type=F32).astype(out)


def after(x, *others):
    return lax.optimization_barrier((x, others))[0]


def back_kernel(left_ref, right_ref, out_ref):
    out_ref[...] = lax.dot_general(
        left_ref[...], right_ref[...], (((1,), (1,)), ((), ())), preferred_element_type=F32
    ).astype(out_ref.dtype)


def matmul_back(left, right):
    (m, depth), n = left.shape, right.shape[0]
    tile = 512 if n % 512 == 0 else 256
    return pl.pallas_call(
        back_kernel,
        grid=(n // tile,),
        in_specs=[
            pl.BlockSpec((m, depth), lambda i: (0, 0)),
            pl.BlockSpec((tile, depth), lambda i: (i, 0)),
        ],
        out_specs=pl.BlockSpec((m, tile), lambda i: (0, i)),
        out_shape=jax.ShapeDtypeStruct((m, n), BF16),
        compiler_params=pltpu.CompilerParams(vmem_limit_bytes=24 * 1024 * 1024),
        cost_estimate=pl.CostEstimate(
            flops=2 * m * n * depth,
            bytes_accessed=2 * (m * depth + n * depth + m * n),
            transcendentals=0,
        ),
    )(left, right)


def shift_core(x):
    n = lax.axis_size("width")
    return lax.ppermute(x, "width", [(i, i ^ 1) for i in range(n)])


def shift_y(x):
    n = lax.axis_size("width")
    return lax.ppermute(x, "width", [(i, (i + 2) % n) for i in range(n)])


def shift_z(x, step):
    n = lax.axis_size("hidden")
    return lax.ppermute(x, "hidden", [(i, (i + step) % n) for i in range(n)])


def shift_dp(x):
    n = lax.axis_size("dp")
    return lax.ppermute(x, "dp", [(i, (i + 1) % n) for i in range(n)])


def add(left, right):
    return left.astype(F32) + right.astype(F32)


def reduce_core(x):
    return add(x[:, 0], shift_core(x[:, 1]))


def reduce_y(x):
    ny = x.shape[0]
    total = x[ny - 1]
    for step in range(ny - 1):
        total = add(x[ny - 2 - step], shift_y(total.astype(BF16)))
    return total


def gather_width(x, ny):
    pieces = [None] * ny
    pieces[0] = x
    for step in range(ny - 1):
        x = shift_y(x)
        pieces[ny - 1 - step] = x
    return pieces


def reduce_hidden(x, step):
    n = len(x)
    at = (-step) % n
    total = x[at]
    for _ in range(n - 1):
        at = (at - step) % n
        total = add(x[at], shift_z(total.astype(BF16), step))
    return total


def gather_hidden(x, step, n, others):
    pieces = [None] * n
    pieces[0] = x
    at = 0
    for _ in range(n - 1):
        at = (at - step) % n
        x = shift_z(x, step)
        if others:
            x, others = after(x, *others), ()
        pieces[at] = x
    return pieces


def coefficients(gate_pre, up_pre, tangent):
    sigmoid_gate = jax.nn.sigmoid(gate_pre)
    first = sigmoid_gate * (1.0 + gate_pre * (1.0 - sigmoid_gate))
    second = sigmoid_gate * (1.0 - sigmoid_gate) * (2.0 + gate_pre * (1.0 - 2.0 * sigmoid_gate))
    hidden = (gate_pre * sigmoid_gate * up_pre).astype(BF16)
    hidden_dot = (first * tangent * up_pre).astype(BF16)
    coeff_first = (first * up_pre).astype(BF16)
    coeff_second = (second * tangent * up_pre).astype(BF16)
    return (hidden, hidden_dot, coeff_first, coeff_second)


def errors(back, back_dot, coeff_first, coeff_second):
    first_f = coeff_first.astype(F32)
    err_grad = (back * first_f).astype(BF16)
    err_hess = (back * coeff_second.astype(F32) + back_dot * first_f).astype(BF16)
    return (err_grad, err_hess)


def on_device(tokens, target, gate_weight, up_weight, down_weight, probe_sign):
    inv_width = 1.0 / math.sqrt(D)
    n_dp = lax.axis_size("dp")
    n_width = lax.axis_size("width")
    nz = lax.axis_size("hidden")
    ny = n_width // 2
    rows, cols = tokens.shape
    ff = gate_weight.shape[1]
    token_scale = 1.0 / math.sqrt(rows * n_dp)
    half = cols // n_dp
    t = rows // CHUNKS
    r = t // (n_width * nz)
    dp = lax.axis_index("dp")
    w = lax.axis_index("width")
    z = lax.axis_index("hidden")

    row = lax.broadcasted_iota(jnp.int32, (rows, rows), 0)
    col = lax.broadcasted_iota(jnp.int32, (rows, rows), 1)
    sz = (row // r) % nz
    pc = (row // (r * nz)) % 2
    py = (row // (r * nz * 2)) % ny
    source = (
        (row // t) * t
        + ((((py + w // 2) % ny) * 2 + (pc + w % 2) % 2) * nz + (sz + z) % nz) * r
        + row % r
    )
    order = (source == col).astype(BF16)
    tokens = matmul(order, tokens)
    target = matmul(order, target)
    mine = lax.dynamic_slice_in_dim(tokens, dp * half, half, 1)
    other = shift_dp(lax.dynamic_slice_in_dim(tokens, (1 - dp) * half, half, 1))

    def stage_a(tok, early, late):
        chip = []
        for weight in (gate_weight, up_weight, probe_sign):
            held = after(tok, *(late if chip else early))
            if len(chip) == 2:
                held = after(held, chip[0])
            chip.append(reduce_core(matmul(held, weight).reshape(ny, 2, nz * r, ff)))
        pre = [reduce_y(part) for part in chip]
        hidden, hidden_dot, c1, c2 = coefficients(pre[0], pre[1], pre[2] * inv_width)
        both = jnp.stack([hidden, hidden_dot])
        own = jnp.stack(gather_width(both, ny), axis=1)
        full = jnp.stack([own, shift_core(own)], axis=2)
        return full.reshape(2 * t, ff), c1, c2, own

    def stage_b(k, out, others):
        out = out.reshape(2, n_width, nz, r, cols)
        result, totals = [], []
        for i, step in ((0, 1), (1, -1)):
            total = reduce_hidden([out[i, :, s] for s in range(nz)], step)
            if i == 0:
                goal = target[k * t:(k + 1) * t].reshape(n_width, nz, r, cols)[:, 0]
                total = total - goal.astype(F32)
            total = total.astype(BF16)
            totals.append(total)
            pieces = gather_hidden(total, step, nz, others)
            result.append(jnp.stack(pieces, axis=1).reshape(t, cols))
        return jnp.concatenate(result), totals

    def stage_c(resid, c1, c2):
        back = matmul_back(resid, down_weight).reshape(2, ny, 2, nz * r, ff)
        return errors(reduce_y(reduce_core(back[0])), reduce_y(reduce_core(back[1])), c1, c2)

    def gather_error(err, y_last):
        own = gather_width(err, ny)
        if y_last:
            far = gather_width(shift_dp(err), ny)
        else:
            far = [shift_dp(piece) for piece in own]
        part = jnp.stack(own + far)
        return jnp.stack([part, shift_core(part)], axis=1).reshape(n_dp * t, ff)

    gathered = []
    early = late = totals = err = ()
    for k in range(CHUNKS):
        full, c1, c2, own = stage_a(tokens[k * t:(k + 1) * t], early, late)
        out = matmul(after(full, *totals), down_weight)
        early, late = (own, other), (out,)
        resid, totals = stage_b(k, out, err)
        err = stage_c(resid, c1, c2)
        gathered.append([gather_error(err[i], k == CHUNKS - 1 and i == 1) for i in range(2)])
    tok = jnp.concatenate(
        [part[k * t:(k + 1) * t] for k in range(CHUNKS) for part in (mine, other)]
    )
    sums = [
        matmul(tok, jnp.concatenate([g[i] for g in gathered]), ((0,), (0,)), F32)
        for i in range(2)
    ]
    probe_rows = lax.dynamic_slice_in_dim(probe_sign, dp * half, half, 0)
    gate_grad = (sums[0] * token_scale).astype(BF16)
    hess_diag = (probe_rows.astype(F32) * (sums[1] * token_scale) * inv_width).astype(BF16)
    return (gate_grad, hess_diag)


def solution(mesh):
    return jax.shard_map(
        on_device,
        mesh=mesh,
        in_specs=(
            P("dp", "width"),
            P("dp", "width"),
            P("width", "hidden"),
            P("width", "hidden"),
            P("hidden", "width"),
            P("width", "hidden"),
        ),
        out_specs=(P(("width", "dp"), "hidden"), P(("width", "dp"), "hidden")),
        check_vma=False,
    )
```
